1024 devices in a mesh: blk: 32 (over x, y_lo, core), dp: 32 (over z, y_hi).
Axes of the slice: x: 8, y: 8 (y_hi: 4, y_lo: 2; y = y_hi * 2 + y_lo), z: 8, core: 2. Of those that a mesh axis runs over, the one named last changes fastest.
Arguments:
- tokens: bfloat16 [8192, 16384], P('dp', 'blk'), may hold values from -6 to 6
- cotangent: bfloat16 [8192, 16384], P('dp', 'blk'), may hold values from -6 to 6
- up_first: bfloat16 [128, 128, 128], P('blk'), may hold values from -0.5 to 0.5
- up_second: bfloat16 [128, 128, 416], P('blk'), may hold values from -0.5 to 0.5
- down_first: bfloat16 [128, 416, 128], P('blk'), may hold values from -0.3125 to 0.3125
- down_second: bfloat16 [128, 128, 128], P('blk'), may hold values from -0.5 to 0.5
Outputs:
- grad_tokens: bfloat16 [8192, 16384], P('dp', 'blk')
- grad_up_first: float32 [128, 128, 128], P('blk', 'dp')
- grad_up_second: float32 [128, 128, 416], P('blk', 'dp')
- grad_down_first: float32 [128, 416, 128], P('blk', 'dp')
- grad_down_second: float32 [128, 128, 128], P('blk', 'dp')
The draws below stay inside these ranges and needn't reach their ends.
All inputs are finite; a program needn't handle non-finite values.
Results may differ from the reference program's by a relative error of at most 0.03.
Values may be sent and summed in bfloat16 or wider, within the bound.
A program may use at most 32 MiB of HBM per device.

```python
import jax
import jax.numpy as jnp
from jax import lax

BS = 128
HB = 416
TOK_DEV = 256
NBLK = 128
D = 16384
TOKENS = 8192
N_DP = 32


def shard_levels(own_key, extent, cuts, least, largest):
    def one(axis_at, parts):
        steps = jax.random.uniform(jax.random.fold_in(jax.random.fold_in(own_key, 6), axis_at), (parts,), jnp.float32, least / len(cuts), largest / len(cuts))
        return jnp.repeat(jnp.exp(steps), extent[axis_at] // parts).reshape((-1,) + (1,) * (len(extent) - axis_at - 1))

    level = one(*cuts[0])
    for cut in cuts[1:]:
        level = level * one(*cut)
    return level


def noise(stream_key, shape, spread, bound, split=(), kind=jnp.bfloat16):
    result = spread * jax.random.normal(stream_key, shape, jnp.float32)
    if split:
        result = result * shard_levels(stream_key, shape, split, -0.22, 0.18)
    return jnp.clip(result, -bound, bound).astype(kind)


def setup_inputs(seed: int = 0) -> dict:
    splits = jax.random.split(jax.random.key(seed), 7)
    tokens = noise(splits[0], (TOKENS, D), 1.0, 6.0, ((0, 32), (1, 32)))
    cotangent = noise(splits[1], (TOKENS, D), 1.0, 6.0, ((0, 32), (1, 32)))
    up_first = noise(splits[2], (NBLK, BS, BS), BS ** -0.5, 0.5, ((0, 32),))
    up_second = noise(splits[3], (NBLK, BS, HB), BS ** -0.5, 0.5, ((0, 32),))
    down_first = noise(splits[4], (NBLK, HB, BS), HB ** -0.5, 0.3125, ((0, 32),))
    down_second = noise(splits[5], (NBLK, BS, BS), BS ** -0.5, 0.5, ((0, 32),))
    return dict(tokens=tokens, cotangent=cotangent, up_first=up_first, up_second=up_second, down_first=down_first, down_second=down_second)


def gelu_tanh(value):
    inner_arg = 0.7978845608 * (value + 0.044715 * value * value * value)
    return 0.5 * value * (1.0 + jnp.tanh(inner_arg))

def gelu_slope(value):
    tangent = jnp.tanh(0.7978845608 * (value + 0.044715 * value * value * value))
    return 0.5 * (1.0 + tangent) + 0.5 * value * (1.0 - tangent * tangent) * 0.7978845608 * (1.0 + 3.0 * 0.044715 * value * value)

def blockwise(acts, weight):
    tok_count = acts.shape[0]
    blocks = acts.reshape(tok_count, NBLK, -1).astype(jnp.float32)
    return jnp.einsum('tbi,bio->tbo', blocks, weight).reshape(tok_count, -1)

def blockwise_back(grads, weight):
    tok_count = grads.shape[0]
    blocks = grads.reshape(tok_count, NBLK, -1).astype(jnp.float32)
    return jnp.einsum('tbo,bio->tbi', blocks, weight).reshape(tok_count, -1)

def block_grad(acts, grads):
    tok_count = acts.shape[0]
    left = acts.reshape(tok_count, NBLK, -1).astype(jnp.float32)
    right = grads.reshape(tok_count, NBLK, -1).astype(jnp.float32)
    return jnp.einsum('tbi,tbo->bio', left, right)

def stride_forward(acts):
    tok_count = acts.shape[0]
    return acts.reshape(tok_count, NBLK, BS).transpose(0, 2, 1).reshape(tok_count, D)

def stride_inverse(acts):
    tok_count = acts.shape[0]
    return acts.reshape(tok_count, BS, NBLK).transpose(0, 2, 1).reshape(tok_count, D)

def reference(tokens, cotangent, up_first, up_second, down_first, down_second):
    up_one = up_first.astype(jnp.float32)
    up_two = up_second.astype(jnp.float32)
    down_one = down_first.astype(jnp.float32)
    down_two = down_second.astype(jnp.float32)
    tok_groups = tokens.reshape(N_DP, TOK_DEV, D)
    cot_groups = cotangent.reshape(N_DP, TOK_DEV, D)

    def group_step(totals, inputs):
        tok_group, cot_group = inputs
        first = blockwise(tok_group, up_one).astype(jnp.bfloat16)
        permuted = stride_forward(first)
        pre_act = blockwise(permuted, up_two)
        activated = gelu_tanh(pre_act).astype(jnp.bfloat16)
        down_out = blockwise(activated, down_one).astype(jnp.bfloat16)
        mixed = stride_forward(down_out)
        grad_mixed = blockwise_back(cot_group, down_two).astype(jnp.bfloat16)
        grad_down = stride_inverse(grad_mixed)
        grad_act = blockwise_back(grad_down, down_one)
        grad_pre = (grad_act * gelu_slope(pre_act)).astype(jnp.bfloat16)
        grad_perm = blockwise_back(grad_pre, up_two).astype(jnp.bfloat16)
        grad_first = stride_inverse(grad_perm)
        grad_group = blockwise_back(grad_first, up_one).astype(jnp.bfloat16)
        terms = (block_grad(tok_group, grad_first), block_grad(permuted, grad_pre), block_grad(activated, grad_down), block_grad(mixed, cot_group))
        return (jax.tree.map(jnp.add, totals, terms), grad_group)
    start = (jnp.zeros((NBLK, BS, BS), jnp.float32), jnp.zeros((NBLK, BS, HB), jnp.float32), jnp.zeros((NBLK, HB, BS), jnp.float32), jnp.zeros((NBLK, BS, BS), jnp.float32))
    totals, grad_groups = lax.scan(group_step, start, (tok_groups, cot_groups))
    factor = TOKENS ** (-0.5)
    return (grad_groups.reshape(TOKENS, D), totals[0] * factor, totals[1] * factor, totals[2] * factor, totals[3] * factor)
```

```python
import functools

import jax
import jax.numpy as jnp
from jax import lax
from jax.experimental import pallas as pl
from jax.experimental.pallas import tpu as pltpu
from jax.sharding import PartitionSpec as P

MESH = pl.DeviceIdType.MESH
F32 = jnp.float32
BF16 = jnp.bfloat16
PAD = 16


def dot(left, right, left_dim=1, right_dim=0):
    return lax.dot_general(
        left, right, (((left_dim,), (right_dim,)), ((), ())), preferred_element_type=F32
    )


def one_hot(shape, target):
    rows = lax.broadcasted_iota(jnp.int32, (shape[0], 1), 0)
    cols = lax.broadcasted_iota(jnp.int32, shape, 1)
    return jnp.where(cols == target(rows), 1.0, 0.0).astype(BF16)


def pick_rows(wide, groups, width):
    group = (lax.broadcasted_iota(jnp.int32, (wide.shape[0], 1), 0) >> 2) & 3
    picked = wide[:, :width]
    for index in range(1, groups):
        picked = jnp.where(group == index, wide[:, index * width : (index + 1) * width], picked)
    return picked


def send_all(axis, count, me, src, dst, send_sem, recv_sem):
    def step(offset, carry):
        target = lax.rem(me + offset, count)
        pltpu.make_async_remote_copy(
            src_ref=src.at[target],
            dst_ref=dst.at[me],
            send_sem=send_sem,
            recv_sem=recv_sem,
            device_id={axis: target},
            device_id_type=MESH,
        ).start()
        return carry

    lax.fori_loop(1, count, step, 0)
    dst[me] = src[me]


def wait_all(count, ref, sem):
    block = ref.at[pl.ds(0, count - 1)]
    pltpu.make_async_copy(block, block, sem).wait()


def kernel(
    blk_count,
    dp_count,
    factor,
    tok,
    cot,
    up_one,
    up_two,
    down_one,
    down_two,
    grad_tok,
    grad_up_one,
    grad_up_two,
    grad_down_one,
    grad_down_two,
    fwd_out,
    fwd_in,
    bwd_out,
    bwd_in,
    send,
    recv,
    early_send,
    early_recv,
    late_send,
    late_recv,
    wide,
    stack,
    perm,
    grad_down,
    tok_flip,
    pre_act,
    activated,
    slope,
    grad_pre,
    grad_two,
    up_wide,
    up_flip,
    down_wide,
    down_flip,
    spread,
    send_sems,
    recv_sems,
):
    groups, size, hidden = up_two.shape
    total = groups * size
    tokens = tok.shape[0]
    bits = size.bit_length() - 1
    unit = hidden // dp_count
    hidden_pad = dp_count * PAD
    me_blk = lax.axis_index("blk")
    me_dp = lax.axis_index("dp")

    barrier = pltpu.get_barrier_semaphore()
    for axis, count, me in (("blk", blk_count, me_blk), ("dp", dp_count, me_dp)):

        def greet(offset, carry, axis=axis, count=count, me=me):
            pl.semaphore_signal(
                barrier,
                inc=1,
                device_id={axis: lax.rem(me + offset, count)},
                device_id_type=MESH,
            )
            return carry

        lax.fori_loop(1, count, greet, 0)

    square = (total, total)
    fwd_out[...] = one_hot(square, lambda r: ((r & 3) << bits) + ((r >> 4) << 2) + ((r >> 2) & 3))
    for b in range(groups):
        cols = pl.ds(b * size, size)
        wide[:, cols] = dot(tok[:, cols], up_one[b]).astype(BF16)
    send[0] = dot(fwd_out[...], wide[...], 1, 1).astype(BF16).reshape(send.shape[1:])
    pl.semaphore_wait(barrier, blk_count + dp_count - 2)
    send_all("blk", blk_count, me_blk, send.at[0], recv.at[0], send_sems.at[0], recv_sems.at[0])

    bwd_out[...] = one_hot(square, lambda r: (((r >> 2) & 3) << bits) + ((r >> 4) << 2) + (r & 3))
    for c in range(groups):
        cols = pl.ds(c * size, size)
        wide[:, cols] = dot(cot[:, cols], down_two[c], 1, 1).astype(BF16)
    send[1] = dot(bwd_out[...], wide[...], 1, 1).astype(BF16).reshape(send.shape[1:])
    send_all("blk", blk_count, me_blk, send.at[1], recv.at[1], send_sems.at[1], recv_sems.at[1])

    low = size - 1
    fwd_in[...] = one_hot(
        square, lambda r: (((r & low) >> 2) << 4) + ((r >> bits) << 2) + (r & 3)
    )
    bwd_in[...] = one_hot(
        square, lambda r: (((r & low) >> 2) << 4) + ((r & 3) << 2) + (r >> bits)
    )
    spread[...] = one_hot(
        (hidden_pad, hidden),
        lambda r: jnp.where((r & (PAD - 1)) < unit, (r >> 4) * unit + (r & (PAD - 1)), -1),
    )
    eye = one_hot((size, size), lambda r: r)
    for c in range(groups):
        up_wide[c] = dot(up_two[c], spread[...], 1, 1).astype(BF16)
        up_flip[c] = dot(spread[...], up_two[c], 1, 1).astype(BF16)
        down_wide[c] = dot(spread[...], down_one[c]).astype(BF16)
        down_flip[c] = dot(eye, down_wide[c], 1, 1).astype(BF16)
    tok_flip[...] = dot(bwd_out[...], tok[...], 1, 1).astype(BF16)

    wait_all(blk_count, recv.at[0], recv_sems.at[0])
    perm[...] = dot(fwd_in[...], recv[0].reshape(total, tokens)).astype(BF16)
    rows_step = 32
    for c in range(groups):
        rows = pl.ds(c * size, size)
        pre_act[...] = dot(up_flip[c], perm[rows, :])

        def gelu(step, carry, c=c):
            part = pl.ds(pl.multiple_of(step * rows_step, rows_step), rows_step)
            value = pre_act[part, :]
            square_value = value * value
            tangent = jnp.tanh(0.7978845608 * (value + 0.044715 * square_value * value))
            half = 0.5 * (1.0 + tangent)
            activated[c, part, :] = (value * half).astype(BF16)
            slope[c, part, :] = half + 0.5 * value * (1.0 - tangent * tangent) * 0.7978845608 * (
                1.0 + 3.0 * 0.044715 * square_value
            )
            return carry

        lax.fori_loop(0, hidden_pad // rows_step, gelu, 0)
        stack[rows, :] = dot(down_flip[c], activated[c]).astype(BF16)
    send[2] = dot(fwd_out[...], stack[...]).astype(BF16).reshape(send.shape[1:])
    send_all("blk", blk_count, me_blk, send.at[2], recv.at[2], send_sems.at[2], recv_sems.at[2])

    wait_all(blk_count, recv.at[1], recv_sems.at[1])
    grad_down[...] = dot(bwd_in[...], recv[1].reshape(total, tokens)).astype(BF16)
    for c in range(groups):
        rows = pl.ds(c * size, size)
        grad_pre[c] = (dot(down_wide[c], grad_down[rows, :]) * slope[c]).astype(BF16)
        stack[rows, :] = dot(up_wide[c], grad_pre[c]).astype(BF16)
    send[3] = dot(bwd_out[...], stack[...]).astype(BF16).reshape(send.shape[1:])
    send_all("blk", blk_count, me_blk, send.at[3], recv.at[3], send_sems.at[3], recv_sems.at[3])

    for c in range(groups):
        rows = pl.ds(c * size, size)
        term = dot(activated[c], grad_down[rows, :], 1, 1).astype(BF16)
        early_send[:, pl.ds(c * PAD, PAD), :] = term.reshape(dp_count, PAD, size)
        grad_two[rows, :] = dot(perm[rows, :], grad_pre[c], 1, 1).astype(BF16)
    mixed_rows = dot(bwd_out[...], grad_two[...]).astype(BF16)
    for tile in range(hidden_pad // size):
        early_send[:, pl.ds((groups + tile) * PAD, PAD), :] = mixed_rows[
            :, tile * size : (tile + 1) * size
        ].reshape(dp_count, PAD, size)
    send_all("dp", dp_count, me_dp, early_send, early_recv, send_sems.at[4], recv_sems.at[4])

    wait_all(blk_count, recv.at[2], recv_sems.at[2])
    every = dot(recv[2].reshape(total, tokens), cot[...])
    late_send[0] = pick_rows(every, groups, size).astype(BF16).reshape(late_send.shape[1:])
    send_all(
        "dp", dp_count, me_dp, late_send.at[0], late_recv.at[0], send_sems.at[5], recv_sems.at[5]
    )

    wait_all(blk_count, recv.at[3], recv_sems.at[3])
    wide[...] = dot(recv[3].reshape(total, tokens), fwd_out[...], 0, 0).astype(BF16)
    every = dot(tok_flip[...], wide[...])
    late_send[1] = pick_rows(every, groups, size).astype(BF16).reshape(late_send.shape[1:])
    send_all(
        "dp", dp_count, me_dp, late_send.at[1], late_recv.at[1], send_sems.at[6], recv_sems.at[6]
    )
    for b in range(groups):
        cols = pl.ds(b * size, size)
        grad_tok[:, cols] = dot(wide[:, cols], up_one[b], 1, 1).astype(BF16)

    wait_all(dp_count, early_recv, recv_sems.at[4])
    for c in range(groups):
        term = jnp.sum(early_recv[:, pl.ds(c * PAD, PAD), :].astype(F32), axis=0) * factor
        grad_down_one[c] = term[:unit]
    tiles = []
    for tile in range(hidden_pad // size):
        part = early_recv[:, pl.ds((groups + tile) * PAD, PAD), :]
        tiles.append(jnp.sum(part.astype(F32), axis=0) * factor)
    summed = jnp.concatenate(tiles, axis=1)
    summed = lax.dot_general(
        summed,
        spread[...].astype(F32),
        (((1,), (0,)), ((), ())),
        precision=lax.Precision.HIGHEST,
        preferred_element_type=F32,
    )
    unit_rows = size // dp_count
    for c in range(groups):
        grad_up_two[c] = summed[c * unit_rows : (c + 1) * unit_rows]
    wait_all(dp_count, late_recv.at[0], recv_sems.at[5])
    term = jnp.sum(late_recv[0].astype(F32), axis=0) * factor
    for c in range(groups):
        grad_down_two[c] = term[c * unit_rows : (c + 1) * unit_rows]
    wait_all(dp_count, late_recv.at[1], recv_sems.at[6])
    term = jnp.sum(late_recv[1].astype(F32), axis=0) * factor
    for c in range(groups):
        grad_up_one[c] = term[c * unit_rows : (c + 1) * unit_rows]

    for index in range(4):
        wait_all(blk_count, send.at[index], send_sems.at[index])
    wait_all(dp_count, early_send, send_sems.at[4])
    for index in range(2):
        wait_all(dp_count, late_send.at[index], send_sems.at[5 + index])


def body(tok, cot, up_one, up_two, down_one, down_two):
    groups, size, hidden = up_two.shape
    tokens = tok.shape[0]
    blk_count = lax.axis_size("blk")
    dp_count = lax.axis_size("dp")
    total = groups * size
    hidden_pad = dp_count * PAD
    unit_rows = size // dp_count
    factor = float(tokens * dp_count) ** (-0.5)
    chunk = groups * groups
    vmem = pl.BlockSpec(memory_space=pltpu.VMEM)
    shapes = [
        ((total, total), BF16),
        ((total, total), BF16),
        ((total, total), BF16),
        ((total, total), BF16),
        ((4, blk_count, chunk, tokens), BF16),
        ((4, blk_count, chunk, tokens), BF16),
        ((dp_count, (groups + hidden_pad // size) * PAD, size), BF16),
        ((dp_count, (groups + hidden_pad // size) * PAD, size), BF16),
        ((2, dp_count, chunk, size), BF16),
        ((2, dp_count, chunk, size), BF16),
        ((tokens, total), BF16),
        ((total, tokens), BF16),
        ((total, tokens), BF16),
        ((total, tokens), BF16),
        ((total, tokens), BF16),
        ((hidden_pad, tokens), F32),
        ((groups, hidden_pad, tokens), BF16),
        ((groups, hidden_pad, tokens), F32),
        ((groups, hidden_pad, tokens), BF16),
        ((total, hidden_pad), BF16),
        ((groups, size, hidden_pad), BF16),
        ((groups, hidden_pad, size), BF16),
        ((groups, hidden_pad, size), BF16),
        ((groups, size, hidden_pad), BF16),
        ((hidden_pad, hidden), BF16),
    ]
    return pl.pallas_call(
        functools.partial(kernel, blk_count, dp_count, factor),
        out_shape=(
            jax.ShapeDtypeStruct((tokens, total), BF16),
            jax.ShapeDtypeStruct((groups, unit_rows, size), F32),
            jax.ShapeDtypeStruct((groups, unit_rows, hidden), F32),
            jax.ShapeDtypeStruct((groups, hidden // dp_count, size), F32),
            jax.ShapeDtypeStruct((groups, unit_rows, size), F32),
        ),
        in_specs=[vmem] * 6,
        out_specs=(vmem,) * 5,
        scratch_shapes=[pltpu.VMEM(shape, kind) for shape, kind in shapes]
        + [pltpu.SemaphoreType.DMA((7,)), pltpu.SemaphoreType.DMA((7,))],
        compiler_params=pltpu.CompilerParams(
            collective_id=0, has_side_effects=True, vmem_limit_bytes=48 * 1024 * 1024
        ),
    )(tok, cot, up_one, up_two, down_one, down_two)


def solution(mesh):
    in_specs = (P("dp", "blk"), P("dp", "blk")) + (P("blk", None, None),) * 4
    out_specs = (P("dp", "blk"),) + (P("blk", "dp", None),) * 4
    return jax.shard_map(body, mesh=mesh, in_specs=in_specs, out_specs=out_specs, check_vma=False)
```

```python
import functools

import jax
import jax.numpy as jnp
from jax import lax
from jax.experimental import pallas as pl
from jax.experimental.pallas import tpu as pltpu
from jax.sharding import PartitionSpec as P

MESH = pl.DeviceIdType.MESH
F32 = jnp.float32
BF16 = jnp.bfloat16
PAD = 16


def dot(left, right, left_dim=1, right_dim=0):
    return lax.dot_general(
        left, right, (((left_dim,), (right_dim,)), ((), ())), preferred_element_type=F32
    )


def one_hot(shape, target):
    rows = lax.broadcasted_iota(jnp.int32, (shape[0], 1), 0)
    cols = lax.broadcasted_iota(jnp.int32, shape, 1)
    return jnp.where(cols == target(rows), 1.0, 0.0).astype(BF16)


def pick_rows(wide, groups, width):
    group = (lax.broadcasted_iota(jnp.int32, (wide.shape[0], 1), 0) >> 2) & 3
    picked = wide[:, :width]
    for index in range(1, groups):
        picked = jnp.where(group == index, wide[:, index * width : (index + 1) * width], picked)
    return picked


def send_all(axis, me, count, peer, src, dst, send_sem, recv_sem):
    def step(offset, carry):
        target = lax.rem(me + offset, count)
        pltpu.make_async_remote_copy(
            src_ref=src(target),
            dst_ref=dst.at[me],
            send_sem=send_sem,
            recv_sem=recv_sem,
            device_id={axis: peer(target)},
            device_id_type=MESH,
        ).start()
        return carry

    lax.fori_loop(1, count, step, 0)
    dst[me] = src(me)[...]


def wait_all(block, sem):
    pltpu.make_async_copy(block, block, sem).wait()


def add_up(ref):
    return jnp.sum(ref[...].astype(F32), axis=0)


def kernel(
    blk_count,
    dp_count,
    factor,
    tok_hbm,
    cot_hbm,
    up_one_hbm,
    up_two_hbm,
    down_one_hbm,
    down_two_hbm,
    grad_tok,
    grad_up_one,
    grad_up_two,
    grad_down_one,
    grad_down_two,
    tok,
    cot,
    up_one,
    up_two,
    down_one,
    down_two,
    fwd_out,
    fwd_in,
    bwd_out,
    bwd_in,
    send,
    recv,
    dn_send,
    dn_recv,
    dn_mid,
    dn_last,
    up_send,
    up_recv,
    up_mid,
    up_last,
    late_send,
    late_recv,
    late_mid,
    late_last,
    wide,
    stack,
    perm,
    grad_down,
    tok_flip,
    pre_act,
    activated,
    slope,
    grad_pre,
    grad_two,
    up_wide,
    up_flip,
    down_wide,
    down_flip,
    spread,
    send_sems,
    recv_sems,
    load_sems,
):
    groups, hidden, size = up_two.shape
    total = groups * size
    tokens = tok.shape[0]
    bits = size.bit_length() - 1
    unit = hidden // dp_count
    hidden_pad = dp_count * PAD
    me_blk = lax.axis_index("blk")
    me_dp = lax.axis_index("dp")

    across = dn_send.shape[1]
    along = dn_send.shape[0]
    me_y = lax.rem(me_dp, across)
    me_z = me_dp // across

    def same(index):
        return index

    def z_peer(index):
        return index * across + me_y

    def y_peer(index):
        return me_z * across + index

    pairs = (
        (tok_hbm, tok),
        (up_one_hbm, up_one),
        (cot_hbm, cot),
        (down_two_hbm, down_two),
        (up_two_hbm, up_two),
        (down_one_hbm, down_one),
    )
    loads = [
        pltpu.make_async_copy(src, dst, load_sems.at[index])
        for index, (src, dst) in enumerate(pairs)
    ]
    loads[0].start()
    loads[1].start()
    barrier = pltpu.get_barrier_semaphore()
    rings = (
        ("blk", me_blk, blk_count, same),
        ("dp", me_z, along, z_peer),
        ("dp", me_y, across, y_peer),
    )
    for axis, me, count, peer in rings:

        def greet(offset, carry, axis=axis, me=me, count=count, peer=peer):
            pl.semaphore_signal(
                barrier,
                inc=1,
                device_id={axis: peer(lax.rem(me + offset, count))},
                device_id_type=MESH,
            )
            return carry

        lax.fori_loop(1, count, greet, 0)
    for load in loads[2:]:
        load.start()

    def exchange(index):
        send_all(
            "blk",
            me_blk,
            blk_count,
            same,
            lambda target: send.at[index, target],
            recv.at[index],
            send_sems.at[index],
            recv_sems.at[index],
        )

    def arrive(index):
        wait_all(recv.at[index, pl.ds(0, blk_count - 1)], recv_sems.at[index])
        return recv[index].reshape(total, tokens)

    square = (total, total)
    fwd_out[...] = one_hot(square, lambda r: ((r & 3) << bits) + ((r >> 4) << 2) + ((r >> 2) & 3))
    loads[0].wait()
    loads[1].wait()
    for b in range(groups):
        cols = pl.ds(b * size, size)
        wide[:, cols] = dot(tok[:, cols], up_one[b]).astype(BF16)
    send[0] = dot(fwd_out[...], wide[...], 1, 1).astype(BF16).reshape(send.shape[1:])
    pl.semaphore_wait(barrier, blk_count + along + across - 3)
    exchange(0)

    bwd_out[...] = one_hot(square, lambda r: (((r >> 2) & 3) << bits) + ((r >> 4) << 2) + (r & 3))
    loads[2].wait()
    loads[3].wait()
    for c in range(groups):
        cols = pl.ds(c * size, size)
        wide[:, cols] = dot(cot[:, cols], down_two[c], 1, 1).astype(BF16)
    send[1] = dot(bwd_out[...], wide[...], 1, 1).astype(BF16).reshape(send.shape[1:])
    exchange(1)

    low = size - 1
    fwd_in[...] = one_hot(
        square, lambda r: (((r & low) >> 2) << 4) + ((r >> bits) << 2) + (r & 3)
    )
    bwd_in[...] = one_hot(
        square, lambda r: (((r & low) >> 2) << 4) + ((r & 3) << 2) + (r >> bits)
    )
    spread[...] = one_hot(
        (hidden_pad, hidden),
        lambda r: jnp.where((r & (PAD - 1)) < unit, (r >> 4) * unit + (r & (PAD - 1)), -1),
    )
    eye = one_hot((size, size), lambda r: r)
    loads[4].wait()
    loads[5].wait()
    for c in range(groups):
        up_flip[c] = dot(spread[...], up_two[c]).astype(BF16)
        up_wide[c] = dot(eye, up_flip[c], 1, 1).astype(BF16)
        down_wide[c] = dot(spread[...], down_one[c]).astype(BF16)
        down_flip[c] = dot(eye, down_wide[c], 1, 1).astype(BF16)
    tok_flip[...] = dot(bwd_out[...], tok[...], 1, 1).astype(BF16)

    perm[...] = dot(fwd_in[...], arrive(0)).astype(BF16)
    rows_step = 32
    for c in range(groups):
        rows = pl.ds(c * size, size)
        pre_act[...] = dot(up_flip[c], perm[rows, :])

        def gelu(step, carry, c=c):
            part = pl.ds(pl.multiple_of(step * rows_step, rows_step), rows_step)
            value = pre_act[part, :]
            square_value = value * value
            tangent = jnp.tanh(0.7978845608 * (value + 0.044715 * square_value * value))
            half = 0.5 * (1.0 + tangent)
            activated[c, part, :] = (value * half).astype(BF16)
            slope[c, part, :] = half + 0.5 * value * (1.0 - tangent * tangent) * 0.7978845608 * (
                1.0 + 3.0 * 0.044715 * square_value
            )
            return carry

        lax.fori_loop(0, hidden_pad // rows_step, gelu, 0)
        stack[rows, :] = dot(down_flip[c], activated[c]).astype(BF16)
    send[2] = dot(fwd_out[...], stack[...]).astype(BF16).reshape(send.shape[1:])
    exchange(2)

    grad_down[...] = dot(bwd_in[...], arrive(1)).astype(BF16)
    for c in range(groups):
        rows = pl.ds(c * size, size)
        grad_pre[c] = (dot(down_wide[c], grad_down[rows, :]) * slope[c]).astype(BF16)
        stack[rows, :] = dot(up_wide[c], grad_pre[c]).astype(BF16)
    send[3] = dot(bwd_out[...], stack[...]).astype(BF16).reshape(send.shape[1:])
    exchange(3)

    for c in range(groups):
        rows = pl.ds(c * size, size)
        term = dot(activated[c], grad_down[rows, :], 1, 1).astype(BF16)
        dn_send[:, :, pl.ds(c * PAD, PAD), :] = term.reshape(along, across, PAD, size)
    send_all(
        "dp",
        me_z,
        along,
        z_peer,
        lambda target: dn_send.at[target],
        dn_recv,
        send_sems.at[4],
        recv_sems.at[4],
    )
    for c in range(groups):
        rows = pl.ds(c * size, size)
        grad_two[rows, :] = dot(perm[rows, :], grad_pre[c], 1, 1).astype(BF16)
    mixed_rows = dot(bwd_out[...], grad_two[...]).astype(BF16)
    tiles = hidden_pad // size
    for tile in range(tiles):
        up_send[:, :, pl.ds(tile * PAD, PAD), :] = mixed_rows[
            :, tile * size : (tile + 1) * size
        ].reshape(along, across, PAD, size)
    send_all(
        "dp",
        me_y,
        across,
        y_peer,
        lambda target: up_send.at[:, target],
        up_recv,
        send_sems.at[5],
        recv_sems.at[5],
    )

    def late(index, every):
        late_send[index] = (
            pick_rows(every, groups, size).astype(BF16).reshape(late_send.shape[1:])
        )
        send_all(
            "dp",
            me_z,
            along,
            z_peer,
            lambda target: late_send.at[index, target],
            late_recv.at[index],
            send_sems.at[6 + index],
            recv_sems.at[6 + index],
        )

    late(0, dot(arrive(2), cot[...]))
    wide[...] = dot(arrive(3), fwd_out[...], 0, 0).astype(BF16)
    late(1, dot(tok_flip[...], wide[...]))
    for b in range(groups):
        cols = pl.ds(b * size, size)
        grad_tok[:, cols] = dot(wide[:, cols], up_one[b], 1, 1).astype(BF16)

    wait_all(dn_recv.at[pl.ds(0, along - 1)], recv_sems.at[4])
    dn_mid[...] = add_up(dn_recv).astype(BF16)
    send_all(
        "dp",
        me_y,
        across,
        y_peer,
        lambda target: dn_mid.at[target],
        dn_last,
        send_sems.at[8],
        recv_sems.at[8],
    )
    wait_all(up_recv.at[pl.ds(0, across - 1)], recv_sems.at[5])
    up_mid[...] = add_up(up_recv).astype(BF16)
    send_all(
        "dp",
        me_z,
        along,
        z_peer,
        lambda target: up_mid.at[target],
        up_last,
        send_sems.at[9],
        recv_sems.at[9],
    )
    for index in range(2):
        wait_all(late_recv.at[index, pl.ds(0, along - 1)], recv_sems.at[6 + index])
        late_mid[:, pl.ds(index * PAD, PAD), :] = add_up(late_recv.at[index]).astype(BF16)
    send_all(
        "dp",
        me_y,
        across,
        y_peer,
        lambda target: late_mid.at[target],
        late_last,
        send_sems.at[10],
        recv_sems.at[10],
    )

    unit_rows = size // dp_count
    wait_all(dn_last.at[pl.ds(0, across - 1)], recv_sems.at[8])
    summed = add_up(dn_last) * factor
    for c in range(groups):
        grad_down_one[:, c, :] = summed[c * PAD : c * PAD + unit]
    wait_all(up_last.at[pl.ds(0, along - 1)], recv_sems.at[9])
    summed = add_up(up_last) * factor
    summed = lax.dot_general(
        jnp.concatenate([summed[tile * PAD : (tile + 1) * PAD] for tile in range(tiles)], axis=1),
        spread[...].astype(F32),
        (((1,), (0,)), ((), ())),
        precision=lax.Precision.HIGHEST,
        preferred_element_type=F32,
    )
    for c in range(groups):
        grad_up_two[c] = summed[c * unit_rows : (c + 1) * unit_rows]
    wait_all(late_last.at[pl.ds(0, across - 1)], recv_sems.at[10])
    summed = add_up(late_last) * factor
    for c in range(groups):
        grad_down_two[c] = summed[c * unit_rows : (c + 1) * unit_rows]
        grad_up_one[c] = summed[PAD + c * unit_rows : PAD + (c + 1) * unit_rows]

    for index in range(4):
        wait_all(send.at[index, pl.ds(0, blk_count - 1)], send_sems.at[index])
    wait_all(dn_send.at[pl.ds(0, along - 1)], send_sems.at[4])
    wait_all(up_send.at[:, pl.ds(0, across - 1)], send_sems.at[5])
    for index in range(2):
        wait_all(late_send.at[index, pl.ds(0, along - 1)], send_sems.at[6 + index])
    wait_all(dn_mid.at[pl.ds(0, across - 1)], send_sems.at[8])
    wait_all(up_mid.at[pl.ds(0, along - 1)], send_sems.at[9])
    wait_all(late_mid.at[pl.ds(0, across - 1)], send_sems.at[10])


def store(*refs):
    count = len(refs) // 2
    copies = [
        pltpu.make_async_copy(refs[index], refs[count + index], refs[-1].at[index])
        for index in range(count)
    ]
    for copy in copies:
        copy.start()
    for copy in copies:
        copy.wait()


def body(tok, cot, up_one, up_two, down_one, down_two):
    groups, size, hidden = up_two.shape
    up_two = jnp.swapaxes(up_two, 1, 2)
    tokens = tok.shape[0]
    blk_count = lax.axis_size("blk")
    dp_count = lax.axis_size("dp")
    total = groups * size
    hidden_pad = dp_count * PAD
    unit_rows = size // dp_count
    factor = float(tokens * dp_count) ** (-0.5)
    chunk = groups * groups
    across = 4 if dp_count % 8 == 0 else 2
    along = dp_count // across
    rows = groups * PAD
    vmem = pl.BlockSpec(memory_space=pltpu.VMEM)
    hbm = pl.BlockSpec(memory_space=pl.ANY)
    shapes = [(arg.shape, BF16) for arg in (tok, cot, up_one, up_two, down_one, down_two)]
    shapes += [
        ((total, total), BF16),
        ((total, total), BF16),
        ((total, total), BF16),
        ((total, total), BF16),
        ((4, blk_count, chunk, tokens), BF16),
        ((4, blk_count, chunk, tokens), BF16),
        ((along, across, rows, size), BF16),
        ((along, across, rows, size), BF16),
        ((across, rows, size), BF16),
        ((across, rows, size), BF16),
        ((along, across, rows, size), BF16),
        ((across, along, rows, size), BF16),
        ((along, rows, size), BF16),
        ((along, rows, size), BF16),
        ((2, along, across, chunk, size), BF16),
        ((2, along, across, chunk, size), BF16),
        ((across, 2 * chunk, size), BF16),
        ((across, 2 * chunk, size), BF16),
        ((tokens, total), BF16),
        ((total, tokens), BF16),
        ((total, tokens), BF16),
        ((total, tokens), BF16),
        ((total, tokens), BF16),
        ((hidden_pad, tokens), F32),
        ((groups, hidden_pad, tokens), BF16),
        ((groups, hidden_pad, tokens), F32),
        ((groups, hidden_pad, tokens), BF16),
        ((total, hidden_pad), BF16),
        ((groups, size, hidden_pad), BF16),
        ((groups, hidden_pad, size), BF16),
        ((groups, hidden_pad, size), BF16),
        ((groups, size, hidden_pad), BF16),
        ((hidden_pad, hidden), BF16),
    ]
    outs = (
        jax.ShapeDtypeStruct((tokens, total), BF16),
        jax.ShapeDtypeStruct((groups, unit_rows, size), F32),
        jax.ShapeDtypeStruct((groups, unit_rows, hidden), F32),
        jax.ShapeDtypeStruct((hidden // dp_count, groups, size), F32),
        jax.ShapeDtypeStruct((groups, unit_rows, size), F32),
    )
    results = pl.pallas_call(
        functools.partial(kernel, blk_count, dp_count, factor),
        out_shape=outs,
        in_specs=[hbm] * 6,
        out_specs=(vmem,) * 5,
        scratch_shapes=[pltpu.VMEM(shape, kind) for shape, kind in shapes]
        + [
            pltpu.SemaphoreType.DMA((11,)),
            pltpu.SemaphoreType.DMA((11,)),
            pltpu.SemaphoreType.DMA((6,)),
        ],
        compiler_params=pltpu.CompilerParams(
            collective_id=0, has_side_effects=True, vmem_limit_bytes=60 * 1024 * 1024
        ),
    )(tok, cot, up_one, up_two, down_one, down_two)
    results = pl.pallas_call(
        store,
        out_shape=outs,
        in_specs=[hbm] * 5,
        out_specs=(hbm,) * 5,
        scratch_shapes=[pltpu.SemaphoreType.DMA((5,))],
        compiler_params=pltpu.CompilerParams(vmem_limit_bytes=60 * 1024 * 1024),
    )(*results)
    results = list(results)
    results[3] = jnp.swapaxes(results[3], 0, 1)
    return tuple(results)


def solution(mesh):
    in_specs = (P("dp", "blk"), P("dp", "blk")) + (P("blk", None, None),) * 4
    out_specs = (P("dp", "blk"),) + (P("blk", "dp", None),) * 4
    return jax.shard_map(body, mesh=mesh, in_specs=in_specs, out_specs=out_specs, check_vma=False)
```

```python
import functools

import jax
import jax.numpy as jnp
from jax import lax
from jax.experimental import pallas as pl
from jax.experimental.pallas import tpu as pltpu
from jax.sharding import PartitionSpec as P

MESH = pl.DeviceIdType.MESH
F32 = jnp.float32
BF16 = jnp.bfloat16
PAD = 16


def dot(left, right, left_dim=1, right_dim=0):
    return lax.dot_general(
        left, right, (((left_dim,), (right_dim,)), ((), ())), preferred_element_type=F32
    )


def one_hot(shape, target):
    rows = lax.broadcasted_iota(jnp.int32, (shape[0], 1), 0)
    cols = lax.broadcasted_iota(jnp.int32, shape, 1)
    return jnp.where(cols == target(rows), 1.0, 0.0).astype(BF16)


def pick_rows(wide, groups, width):
    group = (lax.broadcasted_iota(jnp.int32, (wide.shape[0], 1), 0) >> 2) & 3
    picked = wide[:, :width]
    for index in range(1, groups):
        picked = jnp.where(group == index, wide[:, index * width : (index + 1) * width], picked)
    return picked


def send_all(axis, me, count, peer, src, dst, send_sem, recv_sem):
    for offset in range(1, count):
        target = lax.rem(me + offset, count)
        pltpu.make_async_remote_copy(
            src_ref=src(target),
            dst_ref=dst.at[me],
            send_sem=send_sem,
            recv_sem=recv_sem,
            device_id={axis: peer(target)},
            device_id_type=MESH,
        ).start()
    dst[me] = src(me)[...]


def wait_all(block, sem):
    pltpu.make_async_copy(block, block, sem).wait()


def add_up(ref):
    return jnp.sum(ref[...].astype(F32), axis=0)


def kernel(
    blk_count,
    dp_count,
    factor,
    tok_hbm,
    cot_hbm,
    up_one_hbm,
    up_two_hbm,
    down_one_hbm,
    down_two_hbm,
    grad_tok,
    grad_up_one,
    grad_up_two,
    grad_down_one,
    grad_down_two,
    tok,
    cot,
    up_one,
    up_two,
    down_one,
    down_two,
    fwd_out,
    fwd_in,
    bwd_out,
    bwd_in,
    send,
    recv,
    dn_send,
    dn_recv,
    dn_mid,
    dn_last,
    up_send,
    up_recv,
    up_mid,
    up_last,
    late_send,
    late_recv,
    late_mid,
    late_last,
    wide,
    stack,
    perm,
    grad_down,
    tok_flip,
    pre_act,
    activated,
    slope,
    grad_pre,
    grad_two,
    up_wide,
    up_flip,
    down_wide,
    down_flip,
    spread,
    send_sems,
    recv_sems,
    load_sems,
):
    groups, hidden, size = up_two.shape
    total = groups * size
    tokens = tok.shape[0]
    bits = size.bit_length() - 1
    unit = hidden // dp_count
    hidden_pad = dp_count * PAD
    me_blk = lax.axis_index("blk")
    me_dp = lax.axis_index("dp")

    across = dn_send.shape[1]
    along = dn_send.shape[0]
    me_y = lax.rem(me_dp, across)
    me_z = me_dp // across

    def same(index):
        return index

    def z_peer(index):
        return index * across + me_y

    def y_peer(index):
        return me_z * across + index

    pairs = (
        (tok_hbm, tok),
        (up_one_hbm, up_one),
        (cot_hbm, cot),
        (down_two_hbm, down_two),
        (up_two_hbm, up_two),
        (down_one_hbm, down_one),
    )
    loads = [
        pltpu.make_async_copy(src, dst, load_sems.at[index])
        for index, (src, dst) in enumerate(pairs)
    ]
    loads[0].start()
    loads[1].start()
    barrier = pltpu.get_barrier_semaphore()
    rings = (
        ("blk", me_blk, blk_count, same),
        ("dp", me_z, along, z_peer),
        ("dp", me_y, across, y_peer),
    )
    for axis, me, count, peer in rings:

        def greet(offset, carry, axis=axis, me=me, count=count, peer=peer):
            pl.semaphore_signal(
                barrier,
                inc=1,
                device_id={axis: peer(lax.rem(me + offset, count))},
                device_id_type=MESH,
            )
            return carry

        lax.fori_loop(1, count, greet, 0)
    for load in loads[2:]:
        load.start()

    def exchange(index):
        send_all(
            "blk",
            me_blk,
            blk_count,
            same,
            lambda target: send.at[index, target],
            recv.at[index],
            send_sems.at[index],
            recv_sems.at[index],
        )

    def arrive(index):
        wait_all(recv.at[index, pl.ds(0, blk_count - 1)], recv_sems.at[index])
        return recv[index].reshape(total, tokens)

    square = (total, total)
    fwd_out[...] = one_hot(square, lambda r: ((r & 3) << bits) + ((r >> 4) << 2) + ((r >> 2) & 3))
    loads[0].wait()
    loads[1].wait()
    for b in range(groups):
        cols = pl.ds(b * size, size)
        wide[:, cols] = dot(tok[:, cols], up_one[b]).astype(BF16)
    send[0] = dot(fwd_out[...], wide[...], 1, 1).astype(BF16).reshape(send.shape[1:])
    pl.semaphore_wait(barrier, blk_count + along + across - 3)
    exchange(0)

    bwd_out[...] = one_hot(square, lambda r: (((r >> 2) & 3) << bits) + ((r >> 4) << 2) + (r & 3))
    loads[2].wait()
    loads[3].wait()
    for c in range(groups):
        cols = pl.ds(c * size, size)
        wide[:, cols] = dot(cot[:, cols], down_two[c], 1, 1).astype(BF16)
    send[1] = dot(bwd_out[...], wide[...], 1, 1).astype(BF16).reshape(send.shape[1:])
    exchange(1)

    low = size - 1
    fwd_in[...] = one_hot(
        square, lambda r: (((r & low) >> 2) << 4) + ((r >> bits) << 2) + (r & 3)
    )
    bwd_in[...] = one_hot(
        square, lambda r: (((r & low) >> 2) << 4) + ((r & 3) << 2) + (r >> bits)
    )
    spread[...] = one_hot(
        (hidden_pad, hidden),
        lambda r: jnp.where((r & (PAD - 1)) < unit, (r >> 4) * unit + (r & (PAD - 1)), -1),
    )
    eye = one_hot((size, size), lambda r: r)
    loads[4].wait()
    loads[5].wait()
    for c in range(groups):
        up_flip[c] = dot(spread[...], up_two[c]).astype(BF16)
        up_wide[c] = dot(eye, up_flip[c], 1, 1).astype(BF16)
        down_wide[c] = dot(spread[...], down_one[c]).astype(BF16)
        down_flip[c] = dot(eye, down_wide[c], 1, 1).astype(BF16)
    tok_flip[...] = dot(bwd_out[...], tok[...], 1, 1).astype(BF16)

    perm[...] = dot(fwd_in[...], arrive(0)).astype(BF16)
    rows_step = 32
    for c in range(groups):
        rows = pl.ds(c * size, size)
        pre_act[...] = dot(up_flip[c], perm[rows, :])

        def gelu(step, carry, c=c):
            part = pl.ds(pl.multiple_of(step * rows_step, rows_step), rows_step)
            value = pre_act[part, :]
            square_value = value * value
            tangent = jnp.tanh(0.7978845608 * (value + 0.044715 * square_value * value))
            half = 0.5 * (1.0 + tangent)
            activated[c, part, :] = (value * half).astype(BF16)
            slope[c, part, :] = half + 0.5 * value * (1.0 - tangent * tangent) * 0.7978845608 * (
                1.0 + 3.0 * 0.044715 * square_value
            )
            return carry

        lax.fori_loop(0, hidden_pad // rows_step, gelu, 0)
        stack[rows, :] = dot(down_flip[c], activated[c]).astype(BF16)
    send[2] = dot(fwd_out[...], stack[...]).astype(BF16).reshape(send.shape[1:])
    exchange(2)

    grad_down[...] = dot(bwd_in[...], arrive(1)).astype(BF16)
    for c in range(groups):
        rows = pl.ds(c * size, size)
        grad_pre[c] = (dot(down_wide[c], grad_down[rows, :]) * slope[c]).astype(BF16)
        stack[rows, :] = dot(up_wide[c], grad_pre[c]).astype(BF16)
    send[3] = dot(bwd_out[...], stack[...]).astype(BF16).reshape(send.shape[1:])
    exchange(3)

    for c in range(groups):
        rows = pl.ds(c * size, size)
        term = dot(activated[c], grad_down[rows, :], 1, 1).astype(BF16)
        dn_send[:, :, pl.ds(c * PAD, PAD), :] = term.reshape(along, across, PAD, size)
    send_all(
        "dp",
        me_z,
        along,
        z_peer,
        lambda target: dn_send.at[target],
        dn_recv,
        send_sems.at[4],
        recv_sems.at[4],
    )
    for c in range(groups):
        rows = pl.ds(c * size, size)
        grad_two[rows, :] = dot(perm[rows, :], grad_pre[c], 1, 1).astype(BF16)
    mixed_rows = dot(bwd_out[...], grad_two[...]).astype(BF16)
    tiles = hidden_pad // size
    for tile in range(tiles):
        up_send[:, :, pl.ds(tile * PAD, PAD), :] = mixed_rows[
            :, tile * size : (tile + 1) * size
        ].reshape(along, across, PAD, size)
    send_all(
        "dp",
        me_y,
        across,
        y_peer,
        lambda target: up_send.at[:, target],
        up_recv,
        send_sems.at[5],
        recv_sems.at[5],
    )

    def late(index, rows):
        late_send[index] = rows.astype(BF16).reshape(late_send.shape[1:])
        send_all(
            "dp",
            me_z,
            along,
            z_peer,
            lambda target: late_send.at[index, target],
            late_recv.at[index],
            send_sems.at[6 + index],
            recv_sems.at[6 + index],
        )

    late(0, pick_rows(dot(arrive(2), cot[...]), groups, size))
    across_row = lax.broadcasted_iota(jnp.int32, square, 0)
    same_group = ((across_row >> 2) & 3) == (lax.broadcasted_iota(jnp.int32, square, 1) & 3)
    squeeze = one_hot((total, size), lambda r: r >> 2)
    got = arrive(3)
    every = jnp.where(same_group, dot(tok_flip[...], got, 1, 1), 0.0).astype(BF16)
    late(1, dot(every, squeeze))
    wide[...] = dot(got, fwd_out[...], 0, 0).astype(BF16)
    for b in range(groups):
        cols = pl.ds(b * size, size)
        grad_tok[:, cols] = dot(wide[:, cols], up_one[b], 1, 1).astype(BF16)

    wait_all(dn_recv.at[pl.ds(0, along - 1)], recv_sems.at[4])
    dn_mid[...] = add_up(dn_recv).astype(BF16)
    send_all(
        "dp",
        me_y,
        across,
        y_peer,
        lambda target: dn_mid.at[target],
        dn_last,
        send_sems.at[8],
        recv_sems.at[8],
    )
    wait_all(up_recv.at[pl.ds(0, across - 1)], recv_sems.at[5])
    up_mid[...] = add_up(up_recv).astype(BF16)
    send_all(
        "dp",
        me_z,
        along,
        z_peer,
        lambda target: up_mid.at[target],
        up_last,
        send_sems.at[9],
        recv_sems.at[9],
    )
    for index in range(2):
        wait_all(late_recv.at[index, pl.ds(0, along - 1)], recv_sems.at[6 + index])
        late_mid[:, pl.ds(index * PAD, PAD), :] = add_up(late_recv.at[index]).astype(BF16)
    send_all(
        "dp",
        me_y,
        across,
        y_peer,
        lambda target: late_mid.at[target],
        late_last,
        send_sems.at[10],
        recv_sems.at[10],
    )

    unit_rows = size // dp_count
    wait_all(dn_last.at[pl.ds(0, across - 1)], recv_sems.at[8])
    summed = add_up(dn_last) * factor
    for c in range(groups):
        grad_down_one[:, c, :] = summed[c * PAD : c * PAD + unit]
    wait_all(up_last.at[pl.ds(0, along - 1)], recv_sems.at[9])
    summed = add_up(up_last) * factor
    summed = lax.dot_general(
        jnp.concatenate([summed[tile * PAD : (tile + 1) * PAD] for tile in range(tiles)], axis=1),
        spread[...].astype(F32),
        (((1,), (0,)), ((), ())),
        precision=lax.Precision.HIGHEST,
        preferred_element_type=F32,
    )
    for c in range(groups):
        grad_up_two[c] = summed[c * unit_rows : (c + 1) * unit_rows]
    wait_all(late_last.at[pl.ds(0, across - 1)], recv_sems.at[10])
    summed = add_up(late_last) * factor
    for c in range(groups):
        grad_down_two[c] = summed[c * unit_rows : (c + 1) * unit_rows]
        grad_up_one[c] = summed[PAD + c * unit_rows : PAD + (c + 1) * unit_rows]

    for index in range(4):
        wait_all(send.at[index, pl.ds(0, blk_count - 1)], send_sems.at[index])
    wait_all(dn_send.at[pl.ds(0, along - 1)], send_sems.at[4])
    wait_all(up_send.at[:, pl.ds(0, across - 1)], send_sems.at[5])
    for index in range(2):
        wait_all(late_send.at[index, pl.ds(0, along - 1)], send_sems.at[6 + index])
    wait_all(dn_mid.at[pl.ds(0, across - 1)], send_sems.at[8])
    wait_all(up_mid.at[pl.ds(0, along - 1)], send_sems.at[9])
    wait_all(late_mid.at[pl.ds(0, across - 1)], send_sems.at[10])


def store(*refs):
    count = len(refs) // 2
    for index in range(count):
        refs[count + index][...] = refs[index][...]


def body(tok, cot, up_one, up_two, down_one, down_two):
    groups, size, hidden = up_two.shape
    up_two = jnp.swapaxes(up_two, 1, 2)
    tokens = tok.shape[0]
    blk_count = lax.axis_size("blk")
    dp_count = lax.axis_size("dp")
    total = groups * size
    hidden_pad = dp_count * PAD
    unit_rows = size // dp_count
    factor = float(tokens * dp_count) ** (-0.5)
    chunk = groups * groups
    across = 4 if dp_count % 8 == 0 else 2
    along = dp_count // across
    rows = groups * PAD
    vmem = pl.BlockSpec(memory_space=pltpu.VMEM)
    hbm = pl.BlockSpec(memory_space=pl.ANY)
    shapes = [(arg.shape, BF16) for arg in (tok, cot, up_one, up_two, down_one, down_two)]
    shapes += [
        ((total, total), BF16),
        ((total, total), BF16),
        ((total, total), BF16),
        ((total, total), BF16),
        ((4, blk_count, chunk, tokens), BF16),
        ((4, blk_count, chunk, tokens), BF16),
        ((along, across, rows, size), BF16),
        ((along, across, rows, size), BF16),
        ((across, rows, size), BF16),
        ((across, rows, size), BF16),
        ((along, across, rows, size), BF16),
        ((across, along, rows, size), BF16),
        ((along, rows, size), BF16),
        ((along, rows, size), BF16),
        ((2, along, across, chunk, size), BF16),
        ((2, along, across, chunk, size), BF16),
        ((across, 2 * chunk, size), BF16),
        ((across, 2 * chunk, size), BF16),
        ((tokens, total), BF16),
        ((total, tokens), BF16),
        ((total, tokens), BF16),
        ((total, tokens), BF16),
        ((total, tokens), BF16),
        ((hidden_pad, tokens), F32),
        ((groups, hidden_pad, tokens), BF16),
        ((groups, hidden_pad, tokens), F32),
        ((groups, hidden_pad, tokens), BF16),
        ((total, hidden_pad), BF16),
        ((groups, size, hidden_pad), BF16),
        ((groups, hidden_pad, size), BF16),
        ((groups, hidden_pad, size), BF16),
        ((groups, size, hidden_pad), BF16),
        ((hidden_pad, hidden), BF16),
    ]
    outs = (
        jax.ShapeDtypeStruct((tokens, total), BF16),
        jax.ShapeDtypeStruct((groups, unit_rows, size), F32),
        jax.ShapeDtypeStruct((groups, unit_rows, hidden), F32),
        jax.ShapeDtypeStruct((hidden // dp_count, groups, size), F32),
        jax.ShapeDtypeStruct((groups, unit_rows, size), F32),
    )
    results = pl.pallas_call(
        functools.partial(kernel, blk_count, dp_count, factor),
        out_shape=outs,
        in_specs=[hbm] * 6,
        out_specs=(vmem,) * 5,
        scratch_shapes=[pltpu.VMEM(shape, kind) for shape, kind in shapes]
        + [
            pltpu.SemaphoreType.DMA((11,)),
            pltpu.SemaphoreType.DMA((11,)),
            pltpu.SemaphoreType.DMA((6,)),
        ],
        compiler_params=pltpu.CompilerParams(
            collective_id=0, has_side_effects=True, vmem_limit_bytes=60 * 1024 * 1024
        ),
    )(tok, cot, up_one, up_two, down_one, down_two)
    results = pl.pallas_call(
        store,
        out_shape=outs,
        compiler_params=pltpu.CompilerParams(vmem_limit_bytes=60 * 1024 * 1024),
    )(*results)
    results = list(results)
    results[3] = jnp.swapaxes(results[3], 0, 1)
    return tuple(results)


def solution(mesh):
    in_specs = (P("dp", "blk"), P("dp", "blk")) + (P("blk", None, None),) * 4
    out_specs = (P("dp", "blk"),) + (P("blk", "dp", None),) * 4
    return jax.shard_map(body, mesh=mesh, in_specs=in_specs, out_specs=out_specs, check_vma=False)
```

```python
import functools

import jax
import jax.numpy as jnp
from jax import lax
from jax.experimental import pallas as pl
from jax.experimental.pallas import tpu as pltpu
from jax.sharding import PartitionSpec as P

MESH = pl.DeviceIdType.MESH
F32 = jnp.float32
BF16 = jnp.bfloat16
PAD = 16


def dot(left, right, left_dim=1, right_dim=0):
    return lax.dot_general(
        left, right, (((left_dim,), (right_dim,)), ((), ())), preferred_element_type=F32
    )


def one_hot(shape, target):
    rows = lax.broadcasted_iota(jnp.int32, (shape[0], 1), 0)
    cols = lax.broadcasted_iota(jnp.int32, shape, 1)
    return jnp.where(cols == target(rows), 1.0, 0.0).astype(BF16)


def pick_rows(wide, groups, width):
    group = (lax.broadcasted_iota(jnp.int32, (wide.shape[0], 1), 0) >> 2) & 3
    picked = wide[:, :width]
    for index in range(1, groups):
        picked = jnp.where(group == index, wide[:, index * width : (index + 1) * width], picked)
    return picked


def send_all(axis, me, count, peer, src, dst, send_sem, recv_sem):
    for offset in sorted(range(1, count), key=lambda hop: -min(hop, count - hop)):
        target = lax.rem(me + offset, count)
        pltpu.make_async_remote_copy(
            src_ref=src(target),
            dst_ref=dst.at[me],
            send_sem=send_sem,
            recv_sem=recv_sem,
            device_id={axis: peer(target)},
            device_id_type=MESH,
        ).start()
    dst[me] = src(me)[...]


def wait_all(block, sem):
    pltpu.make_async_copy(block, block, sem).wait()


def add_up(ref):
    return jnp.sum(ref[...].astype(F32), axis=0)


def kernel(
    blk_count,
    dp_count,
    factor,
    tok_hbm,
    cot_hbm,
    up_one_hbm,
    up_two_hbm,
    down_one_hbm,
    down_two_hbm,
    grad_tok,
    grad_up_one,
    grad_up_two,
    grad_down_one,
    grad_down_two,
    tok,
    cot,
    up_one,
    up_two,
    down_one,
    down_two,
    fwd_out,
    fwd_in,
    bwd_out,
    bwd_in,
    send,
    recv,
    dn_send,
    dn_recv,
    dn_mid,
    dn_last,
    up_send,
    up_recv,
    up_mid,
    up_last,
    late_send,
    late_recv,
    late_mid,
    late_last,
    wide,
    stack,
    perm,
    grad_down,
    tok_flip,
    pre_act,
    activated,
    slope,
    grad_pre,
    grad_two,
    up_wide,
    up_flip,
    down_wide,
    down_flip,
    spread,
    tok_out,
    send_sems,
    recv_sems,
    load_sems,
):
    groups, hidden, size = up_two.shape
    total = groups * size
    tokens = tok.shape[0]
    bits = size.bit_length() - 1
    unit = hidden // dp_count
    hidden_pad = dp_count * PAD
    me_blk = lax.axis_index("blk")
    me_dp = lax.axis_index("dp")

    across = dn_send.shape[1]
    along = dn_send.shape[0]
    me_y = lax.rem(me_dp, across)
    me_z = me_dp // across

    def same(index):
        return index

    def z_peer(index):
        return index * across + me_y

    def y_peer(index):
        return me_z * across + index

    pairs = (
        (tok_hbm, tok),
        (up_one_hbm, up_one),
        (cot_hbm, cot),
        (down_two_hbm, down_two),
        (up_two_hbm, up_two),
        (down_one_hbm, down_one),
    )
    loads = [
        pltpu.make_async_copy(src, dst, load_sems.at[index])
        for index, (src, dst) in enumerate(pairs)
    ]
    loads[0].start()
    loads[1].start()
    barrier = pltpu.get_barrier_semaphore()
    rings = (
        ("blk", me_blk, blk_count, same),
        ("dp", me_z, along, z_peer),
        ("dp", me_y, across, y_peer),
    )
    for axis, me, count, peer in rings:

        def greet(offset, carry, axis=axis, me=me, count=count, peer=peer):
            pl.semaphore_signal(
                barrier,
                inc=1,
                device_id={axis: peer(lax.rem(me + offset, count))},
                device_id_type=MESH,
            )
            return carry

        lax.fori_loop(1, count, greet, 0)
    for load in loads[2:]:
        load.start()

    def exchange(index):
        send_all(
            "blk",
            me_blk,
            blk_count,
            same,
            lambda target: send.at[index, target],
            recv.at[index],
            send_sems.at[index],
            recv_sems.at[index],
        )

    def arrive(index):
        wait_all(recv.at[index, pl.ds(0, blk_count - 1)], recv_sems.at[index])
        return recv[index].reshape(total, tokens)

    square = (total, total)
    fwd_out[...] = one_hot(square, lambda r: ((r & 3) << bits) + ((r >> 4) << 2) + ((r >> 2) & 3))
    loads[0].wait()
    loads[1].wait()
    for b in range(groups):
        cols = pl.ds(b * size, size)
        wide[:, cols] = dot(tok[:, cols], up_one[b]).astype(BF16)
    send[0] = dot(fwd_out[...], wide[...], 1, 1).astype(BF16).reshape(send.shape[1:])
    pl.semaphore_wait(barrier, blk_count + along + across - 3)
    exchange(0)

    bwd_out[...] = one_hot(square, lambda r: (((r >> 2) & 3) << bits) + ((r >> 4) << 2) + (r & 3))
    loads[2].wait()
    loads[3].wait()
    for c in range(groups):
        cols = pl.ds(c * size, size)
        wide[:, cols] = dot(cot[:, cols], down_two[c], 1, 1).astype(BF16)
    send[1] = dot(bwd_out[...], wide[...], 1, 1).astype(BF16).reshape(send.shape[1:])
    exchange(1)

    low = size - 1
    fwd_in[...] = one_hot(
        square, lambda r: (((r & low) >> 2) << 4) + ((r >> bits) << 2) + (r & 3)
    )
    bwd_in[...] = one_hot(
        square, lambda r: (((r & low) >> 2) << 4) + ((r & 3) << 2) + (r >> bits)
    )
    spread[...] = one_hot(
        (hidden_pad, hidden),
        lambda r: jnp.where((r & (PAD - 1)) < unit, (r >> 4) * unit + (r & (PAD - 1)), -1),
    )
    eye = one_hot((size, size), lambda r: r)
    loads[4].wait()
    loads[5].wait()
    for c in range(groups):
        up_flip[c] = dot(spread[...], up_two[c]).astype(BF16)
        up_wide[c] = dot(eye, up_flip[c], 1, 1).astype(BF16)
        down_wide[c] = dot(spread[...], down_one[c]).astype(BF16)
        down_flip[c] = dot(eye, down_wide[c], 1, 1).astype(BF16)
    tok_flip[...] = dot(bwd_out[...], tok[...], 1, 1).astype(BF16)

    perm[...] = dot(fwd_in[...], arrive(0)).astype(BF16)
    rows_step = 32
    for c in range(groups):
        rows = pl.ds(c * size, size)
        pre_act[...] = dot(up_flip[c], perm[rows, :])

        def gelu(step, carry, c=c):
            part = pl.ds(pl.multiple_of(step * rows_step, rows_step), rows_step)
            value = pre_act[part, :]
            square_value = value * value
            tangent = jnp.tanh(0.7978845608 * (value + 0.044715 * square_value * value))
            half = 0.5 * (1.0 + tangent)
            activated[c, part, :] = (value * half).astype(BF16)
            slope[c, part, :] = half + 0.5 * value * (1.0 - tangent * tangent) * 0.7978845608 * (
                1.0 + 3.0 * 0.044715 * square_value
            )
            return carry

        lax.fori_loop(0, hidden_pad // rows_step, gelu, 0)
        stack[rows, :] = dot(down_flip[c], activated[c]).astype(BF16)
    send[2] = dot(fwd_out[...], stack[...]).astype(BF16).reshape(send.shape[1:])
    exchange(2)

    grad_down[...] = dot(bwd_in[...], arrive(1)).astype(BF16)
    for c in range(groups):
        rows = pl.ds(c * size, size)
        grad_pre[c] = (dot(down_wide[c], grad_down[rows, :]) * slope[c]).astype(BF16)
        stack[rows, :] = dot(up_wide[c], grad_pre[c]).astype(BF16)
    send[3] = dot(bwd_out[...], stack[...]).astype(BF16).reshape(send.shape[1:])
    exchange(3)

    for c in range(groups):
        rows = pl.ds(c * size, size)
        term = dot(activated[c], grad_down[rows, :], 1, 1).astype(BF16)
        dn_send[:, :, pl.ds(c * PAD, PAD), :] = term.reshape(along, across, PAD, size)
    send_all(
        "dp",
        me_z,
        along,
        z_peer,
        lambda target: dn_send.at[target],
        dn_recv,
        send_sems.at[4],
        recv_sems.at[4],
    )
    for c in range(groups):
        rows = pl.ds(c * size, size)
        grad_two[rows, :] = dot(perm[rows, :], grad_pre[c], 1, 1).astype(BF16)
    mixed_rows = dot(bwd_out[...], grad_two[...]).astype(BF16)
    tiles = hidden_pad // size
    for tile in range(tiles):
        up_send[:, :, pl.ds(tile * PAD, PAD), :] = mixed_rows[
            :, tile * size : (tile + 1) * size
        ].reshape(along, across, PAD, size)
    send_all(
        "dp",
        me_y,
        across,
        y_peer,
        lambda target: up_send.at[:, target],
        up_recv,
        send_sems.at[5],
        recv_sems.at[5],
    )

    def late(index, rows):
        late_send[index] = rows.astype(BF16).reshape(late_send.shape[1:])
        send_all(
            "dp",
            me_z,
            along,
            z_peer,
            lambda target: late_send.at[index, target],
            late_recv.at[index],
            send_sems.at[6 + index],
            recv_sems.at[6 + index],
        )

    late(0, pick_rows(dot(arrive(2), cot[...]), groups, size))
    across_row = lax.broadcasted_iota(jnp.int32, square, 0)
    same_group = ((across_row >> 2) & 3) == (lax.broadcasted_iota(jnp.int32, square, 1) & 3)
    squeeze = one_hot((total, size), lambda r: r >> 2)
    got = arrive(3)
    every = jnp.where(same_group, dot(tok_flip[...], got, 1, 1), 0.0).astype(BF16)
    late(1, dot(every, squeeze))
    wide[...] = dot(got, fwd_out[...], 0, 0).astype(BF16)
    for b in range(groups):
        cols = pl.ds(b * size, size)
        tok_out[:, cols] = dot(wide[:, cols], up_one[b], 1, 1).astype(BF16)
    tok_store = pltpu.make_async_copy(tok_out, grad_tok, load_sems.at[6])
    tok_store.start()

    wait_all(dn_recv.at[pl.ds(0, along - 1)], recv_sems.at[4])
    dn_mid[...] = add_up(dn_recv).astype(BF16)
    send_all(
        "dp",
        me_y,
        across,
        y_peer,
        lambda target: dn_mid.at[target],
        dn_last,
        send_sems.at[8],
        recv_sems.at[8],
    )
    wait_all(up_recv.at[pl.ds(0, across - 1)], recv_sems.at[5])
    up_mid[...] = add_up(up_recv).astype(BF16)
    send_all(
        "dp",
        me_z,
        along,
        z_peer,
        lambda target: up_mid.at[target],
        up_last,
        send_sems.at[9],
        recv_sems.at[9],
    )
    for index in range(2):
        wait_all(late_recv.at[index, pl.ds(0, along - 1)], recv_sems.at[6 + index])
        late_mid[:, pl.ds(index * PAD, PAD), :] = add_up(late_recv.at[index]).astype(BF16)
    send_all(
        "dp",
        me_y,
        across,
        y_peer,
        lambda target: late_mid.at[target],
        late_last,
        send_sems.at[10],
        recv_sems.at[10],
    )

    unit_rows = size // dp_count
    wait_all(dn_last.at[pl.ds(0, across - 1)], recv_sems.at[8])
    summed = add_up(dn_last) * factor
    for c in range(groups):
        grad_down_one[:, c, :] = summed[c * PAD : c * PAD + unit]
    wait_all(up_last.at[pl.ds(0, along - 1)], recv_sems.at[9])
    summed = add_up(up_last) * factor
    summed = lax.dot_general(
        jnp.concatenate([summed[tile * PAD : (tile + 1) * PAD] for tile in range(tiles)], axis=1),
        spread[...].astype(F32),
        (((1,), (0,)), ((), ())),
        precision=lax.Precision.HIGHEST,
        preferred_element_type=F32,
    )
    for c in range(groups):
        grad_up_two[c] = summed[c * unit_rows : (c + 1) * unit_rows]
    wait_all(late_last.at[pl.ds(0, across - 1)], recv_sems.at[10])
    summed = add_up(late_last) * factor
    for c in range(groups):
        grad_down_two[c] = summed[c * unit_rows : (c + 1) * unit_rows]
        grad_up_one[c] = summed[PAD + c * unit_rows : PAD + (c + 1) * unit_rows]

    for index in range(4):
        wait_all(send.at[index, pl.ds(0, blk_count - 1)], send_sems.at[index])
    wait_all(dn_send.at[pl.ds(0, along - 1)], send_sems.at[4])
    wait_all(up_send.at[:, pl.ds(0, across - 1)], send_sems.at[5])
    for index in range(2):
        wait_all(late_send.at[index, pl.ds(0, along - 1)], send_sems.at[6 + index])
    wait_all(dn_mid.at[pl.ds(0, across - 1)], send_sems.at[8])
    wait_all(up_mid.at[pl.ds(0, along - 1)], send_sems.at[9])
    wait_all(late_mid.at[pl.ds(0, across - 1)], send_sems.at[10])
    tok_store.wait()


def store(*refs):
    count = len(refs) // 2
    for index in range(count):
        refs[count + index][...] = refs[index][...]


def body(tok, cot, up_one, up_two, down_one, down_two):
    groups, size, hidden = up_two.shape
    up_two = jnp.swapaxes(up_two, 1, 2)
    tokens = tok.shape[0]
    blk_count = lax.axis_size("blk")
    dp_count = lax.axis_size("dp")
    total = groups * size
    hidden_pad = dp_count * PAD
    unit_rows = size // dp_count
    factor = float(tokens * dp_count) ** (-0.5)
    chunk = groups * groups
    across = 4 if dp_count % 8 == 0 else 2
    along = dp_count // across
    rows = groups * PAD
    vmem = pl.BlockSpec(memory_space=pltpu.VMEM)
    hbm = pl.BlockSpec(memory_space=pl.ANY)
    shapes = [(arg.shape, BF16) for arg in (tok, cot, up_one, up_two, down_one, down_two)]
    shapes += [
        ((total, total), BF16),
        ((total, total), BF16),
        ((total, total), BF16),
        ((total, total), BF16),
        ((4, blk_count, chunk, tokens), BF16),
        ((4, blk_count, chunk, tokens), BF16),
        ((along, across, rows, size), BF16),
        ((along, across, rows, size), BF16),
        ((across, rows, size), BF16),
        ((across, rows, size), BF16),
        ((along, across, rows, size), BF16),
        ((across, along, rows, size), BF16),
        ((along, rows, size), BF16),
        ((along, rows, size), BF16),
        ((2, along, across, chunk, size), BF16),
        ((2, along, across, chunk, size), BF16),
        ((across, 2 * chunk, size), BF16),
        ((across, 2 * chunk, size), BF16),
        ((tokens, total), BF16),
        ((total, tokens), BF16),
        ((total, tokens), BF16),
        ((total, tokens), BF16),
        ((total, tokens), BF16),
        ((hidden_pad, tokens), F32),
        ((groups, hidden_pad, tokens), BF16),
        ((groups, hidden_pad, tokens), F32),
        ((groups, hidden_pad, tokens), BF16),
        ((total, hidden_pad), BF16),
        ((groups, size, hidden_pad), BF16),
        ((groups, hidden_pad, size), BF16),
        ((groups, hidden_pad, size), BF16),
        ((groups, size, hidden_pad), BF16),
        ((hidden_pad, hidden), BF16),
        ((tokens, total), BF16),
    ]
    outs = (
        jax.ShapeDtypeStruct((tokens, total), BF16),
        jax.ShapeDtypeStruct((groups, unit_rows, size), F32),
        jax.ShapeDtypeStruct((groups, unit_rows, hidden), F32),
        jax.ShapeDtypeStruct((hidden // dp_count, groups, size), F32),
        jax.ShapeDtypeStruct((groups, unit_rows, size), F32),
    )
    results = pl.pallas_call(
        functools.partial(kernel, blk_count, dp_count, factor),
        out_shape=outs,
        in_specs=[hbm] * 6,
        out_specs=(hbm,) + (vmem,) * 4,
        scratch_shapes=[pltpu.VMEM(shape, kind) for shape, kind in shapes]
        + [
            pltpu.SemaphoreType.DMA((11,)),
            pltpu.SemaphoreType.DMA((11,)),
            pltpu.SemaphoreType.DMA((7,)),
        ],
        compiler_params=pltpu.CompilerParams(
            collective_id=0, has_side_effects=True, vmem_limit_bytes=60 * 1024 * 1024
        ),
    )(tok, cot, up_one, up_two, down_one, down_two)
    results = pl.pallas_call(
        store,
        out_shape=outs,
        compiler_params=pltpu.CompilerParams(vmem_limit_bytes=60 * 1024 * 1024),
    )(*results)
    results = list(results)
    results[3] = jnp.swapaxes(results[3], 0, 1)
    return tuple(results)


def solution(mesh):
    in_specs = (P("dp", "blk"), P("dp", "blk")) + (P("blk", None, None),) * 4
    out_specs = (P("dp", "blk"),) + (P("blk", "dp", None),) * 4
    return jax.shard_map(body, mesh=mesh, in_specs=in_specs, out_specs=out_specs, check_vma=False)
```
